32 devices in a mesh: seq: 16 (over z, y, core), head: 2 (over x).
Axes of the slice: x: 2, y: 2, z: 4, core: 2. Of those that a mesh axis runs over, the one named last changes fastest.
Arguments:
- queries: bfloat16 [8192, 4096], P(('seq', 'head')), may hold values from -6 to 6
- keys: bfloat16 [8192, 4096], P(('seq', 'head')), may hold values from -6 to 6
- values: bfloat16 [8192, 4096], P(('seq', 'head')), may hold values from -6 to 6
- cluster_ids: int32 [32, 8192, 1], P(None, 'seq'), may hold values from 0 to 127; in each aligned block of 256 rows (0 to 255, 256 to 511, ..., all dimensions but the last counted through in order) at most 4 rows name the same one
- out_weight: bfloat16 [4096, 4096], P('head', 'seq'), may hold values from -0.09375 to 0.09375
Outputs:
- projected: bfloat16 [8192, 4096], P('seq', 'head')
The draws below stay inside these ranges and needn't reach their ends.
Inputs may be any that keep to these rules, and one draw needn't show every extreme that they name: `cluster_ids`: in each aligned block of 256 tokens of one head (the rows of one device), no cluster id appears more than 4 times, and some cluster appears exactly 4 times.
All inputs are finite; a program needn't handle non-finite values.
Results may differ from the reference program's by a relative error of at most 0.014.
Values may be sent and summed in bfloat16 or wider, within the bound.
A program may use at most 128 MiB of HBM per device.

```python
import math
import jax
import jax.numpy as jnp
import numpy as np
from jax import lax

D = 4096
HEADS = 32
HD = 128
CLUSTERS = 128
TOKENS = 8192
SUB = 256
MOST = 4
CAP = 128


def draw_queries(key, part):
    subkey = jax.random.fold_in(key, 101)
    return jnp.clip(jax.random.normal(subkey, (TOKENS, D), jnp.float32), -4.0, 4.0).astype(jnp.bfloat16)


def draw_keys(key, part):
    subkey = jax.random.fold_in(key, 202)
    return jnp.clip(jax.random.normal(subkey, (TOKENS, D), jnp.float32), -4.0, 4.0).astype(jnp.bfloat16)


def shard_levels(own_key, extent, split, low, largest):
    level, own = 1.0, jax.random.fold_in(own_key, 6)
    for dim, parts in split:
        steps = jnp.exp(jax.random.uniform(jax.random.fold_in(own, dim), (parts,), jnp.float32, low / len(split), largest / len(split)))
        level = level * jnp.repeat(steps, extent[dim] // parts).reshape([-1 if axis == dim else 1 for axis in range(len(extent))])
    return level


def shared_out(stream_key, own, number, rows, number_of, top, bound, skew):
    order = jax.random.permutation(stream_key, number_of)
    heavy_load, usual = portions_of(number_of, rows * top, bound, skew, True), portions_of(number_of, rows * top, bound, skew, False)
    places = jnp.arange(number_of)

    def named(tallies, rotation):
        used = int((tallies > 0).sum())
        fixed = max(1, used // 4)
        shifted = fixed + (places - fixed + rotation * (used - fixed)) % max(1, number_of - fixed)
        return jnp.zeros((number_of,), jnp.int32).at[order[jnp.where(places < fixed, places, shifted)]].set(jnp.asarray(tallies, jnp.int32))

    tallies = jnp.where(number % 4 == 0, named(heavy_load, number // 4), named(usual, number - number // 4 - 1))
    mixed = jax.random.permutation(jax.random.fold_in(own, 3), number_of)
    giver, sink = mixed[0:number_of // 2 * 2:2], mixed[1:number_of // 2 * 2:2]
    room = jnp.minimum(tallies[giver] - 1, bound - tallies[sink]) // 2
    room = jnp.where((giver == order[0]) | (sink == order[0]) | (tallies[sink] == 0), 0, jnp.maximum(room, 0))
    shifted = jax.random.randint(jax.random.fold_in(own, 4), (number_of // 2,), 0, 1 << 20) % (room + 1)
    tallies = tallies.at[giver].add(-shifted).at[sink].add(shifted)
    labels = jnp.searchsorted(jnp.cumsum(tallies), jnp.arange(rows * top), side="right").astype(jnp.int32)
    grid = labels.reshape(top, rows).T
    grid = grid[jax.random.permutation(jax.random.fold_in(own, 1), rows)]
    rotation = jax.random.randint(jax.random.fold_in(own, 2), (rows, 1), 0, top)
    return jnp.take_along_axis(grid, (jnp.arange(top)[None, :] + rotation) % top, axis=1)


def portions_of(count, total, most, slope, full):
    weights = [(1 << 20) // math.isqrt(rank ** slope) + 1 for rank in range(1, count + 1)]
    largest = most if full else min(most, max(-(-total // count), total * weights[0] // sum(weights)))
    least = 1 if total - largest >= count - 1 else 0
    given, rest = [largest] + [least] * (count - 1), total - largest - least * (count - 1)
    while rest > 0:
        candidates = [i for i in range(1, count) if given[i] < largest] or [i for i in range(1, count) if given[i] < most]
        whole, remaining = sum([weights[i] for i in candidates]), rest
        for i in candidates:
            more = min(most - given[i], max(1, remaining * weights[i] // whole), rest)
            given[i] = given[i] + more
            rest = rest - more
    return np.array(given)


def centred(stream_key, dims, deviation, bound, shards=(), kind=jnp.bfloat16):
    values = jax.random.normal(stream_key, dims, jnp.float32) * deviation
    if len(shards) > 0:
        values = shard_levels(stream_key, dims, shards, -0.22, 0.18) * values
    return jnp.clip(values, min=-bound, max=bound).astype(kind)


def setup_inputs(seed: int = 0) -> dict:
    splits = jax.random.split(jax.random.key(seed), 6)
    queries = draw_queries(jax.random.fold_in(splits[5], 71), 0)
    keys = draw_keys(jax.random.fold_in(splits[5], 71), 0)
    values = centred(splits[2], (TOKENS, D), 1.0, 6.0, ((0, 32),))
    cluster_ids_keys = jax.random.split(jax.random.fold_in(splits[3], 1), HEADS * TOKENS // SUB)
    cluster_ids_turns = jax.random.permutation(jax.random.fold_in(splits[3], 3), HEADS * TOKENS // SUB)
    cluster_ids = jax.vmap(lambda own, number: shared_out(jax.random.fold_in(splits[3], 2), own, number, SUB, CLUSTERS, 1, MOST, 2))(cluster_ids_keys, cluster_ids_turns).reshape((HEADS, TOKENS, 1))
    out_weight = centred(splits[4], (D, D), D ** -0.5, 0.09375, ((0, 2), (1, 16)))
    return dict(queries=queries, keys=keys, values=values, cluster_ids=cluster_ids, out_weight=out_weight)


def attend_head(inputs):
    query_head, key_head, value_head, head_ids = inputs
    cluster_range = jnp.arange(CLUSTERS, dtype=jnp.int32)
    counts = jnp.sum((head_ids[None, :] == cluster_range[:, None]).astype(jnp.int32), axis=1).astype(jnp.int32)
    starts = (jnp.cumsum(counts) - counts).astype(jnp.int32)
    ordering = jnp.argsort(head_ids, stable=True).astype(jnp.int32)
    sorted_ids = head_ids[ordering]
    position = jnp.arange(TOKENS, dtype=jnp.int32) - starts[sorted_ids]
    target = (sorted_ids * CAP + position).astype(jnp.int32)

    def place_rows(tensor):
        filled = jnp.zeros((CLUSTERS * CAP, HD), tensor.dtype).at[target].set(tensor[ordering])
        return filled.reshape(CLUSTERS, CAP, HD)

    query_block = place_rows(query_head)
    key_block = place_rows(key_head)
    value_block = place_rows(value_head)
    validity = jnp.arange(CAP, dtype=jnp.int32)[None, :] < counts[:, None]
    scores = jnp.einsum('cqd,ckd->cqk', query_block.astype(jnp.float32), key_block.astype(jnp.float32)) * (HD ** -0.5)
    scores = jnp.where(validity[:, None, :], scores, -1.0e30)
    row_max = jnp.max(scores, axis=-1, keepdims=True)
    raised = jnp.exp(scores - row_max)
    weights = (raised / jnp.sum(raised, axis=-1, keepdims=True)).astype(jnp.bfloat16)
    out_block = jnp.einsum('cqk,ckd->cqd', weights.astype(jnp.float32), value_block.astype(jnp.float32)).astype(jnp.bfloat16)
    flat_rows = out_block.reshape(CLUSTERS * CAP, HD)[target]
    return jnp.zeros((TOKENS, HD), jnp.bfloat16).at[ordering].set(flat_rows)


def split_heads(tensor):
    return tensor.reshape(TOKENS, HEADS, HD).transpose(1, 0, 2)


def reference(queries, keys, values, cluster_ids, out_weight):
    per_head = lax.map(attend_head, (split_heads(queries), split_heads(keys), split_heads(values), cluster_ids[:, :, 0]))
    attended = per_head.transpose(1, 0, 2).reshape(TOKENS, D)
    return jnp.dot(attended, out_weight, preferred_element_type=jnp.float32).astype(jnp.bfloat16)
```

```python
import jax
import jax.numpy as jnp
from jax import lax
from jax.sharding import PartitionSpec as P

HEADS = 32
HD = 128
CLUSTERS = 128


def slot_table(block_ids, slot_depth):
    sub_rows = block_ids.shape[-1]
    onehot = (block_ids[..., None] == jnp.arange(CLUSTERS, dtype=jnp.int32)).astype(jnp.float32)
    lower = (jnp.arange(sub_rows)[:, None] >= jnp.arange(sub_rows)[None, :]).astype(jnp.float32)
    running = jnp.einsum("ts,abse->abte", lower, onehot)
    ranking = (jnp.sum(running * onehot, axis=-1) - 1.0).astype(jnp.int32)
    depth_hit = (ranking[..., None] == jnp.arange(slot_depth, dtype=jnp.int32)).astype(jnp.bfloat16)
    return onehot.astype(jnp.bfloat16)[..., :, None] * depth_hit[..., None, :]


def attend_blocks(packed, validity):
    scores = jnp.einsum(
        "cqd,ckd->cqk", packed[0], packed[1], preferred_element_type=jnp.float32
    ) * HD ** (-0.5)
    scores = jnp.where(validity[:, None, :] > 0, scores, -1e30)
    row_max = jnp.max(scores, axis=-1, keepdims=True)
    raised = jnp.exp(scores - row_max)
    weights = (raised / jnp.sum(raised, axis=-1, keepdims=True)).astype(jnp.bfloat16)
    return jnp.einsum(
        "cqk,ckd->cqd", weights, packed[2], preferred_element_type=jnp.float32
    ).astype(jnp.bfloat16)


def attend_and_return(arrived):
    packed, markers = arrived
    item_count = packed.shape[1]
    n_seq = packed.shape[2]
    lane_count = packed.shape[3]
    result_block = attend_blocks(
        packed.reshape(3, item_count, n_seq * lane_count, HD),
        markers.reshape(item_count, n_seq * lane_count),
    )
    result_block = result_block.reshape(item_count, n_seq, lane_count, HD)
    return lax.all_to_all(result_block, "seq", split_axis=1, concat_axis=1, tiled=True)


def generic_body(queries, keys, values, cluster_ids, out_weight):
    n_seq = lax.axis_size("seq")
    n_head = lax.axis_size("head")
    head_group = lax.axis_index("head")
    tok_dev = cluster_ids.shape[1]
    sub_rows = tok_dev // n_head
    group_heads = HEADS // n_head
    slot_depth = max(2, 2 * tok_dev // (n_head * CLUSTERS))
    lane_count = n_head * slot_depth
    per_owner = group_heads * CLUSTERS // n_seq
    all_ids = cluster_ids[:, :, 0]
    group_ids = lax.dynamic_slice_in_dim(all_ids, head_group * group_heads, group_heads, 0)
    group_ids = group_ids.reshape(group_heads, n_head, sub_rows)
    home_table = slot_table(group_ids, slot_depth)
    relaid = (
        lax.all_to_all(queries, "head", split_axis=1, concat_axis=0, tiled=True),
        lax.all_to_all(keys, "head", split_axis=1, concat_axis=0, tiled=True),
        lax.all_to_all(values, "head", split_axis=1, concat_axis=0, tiled=True),
    )
    stacked = jnp.stack([tensor.reshape(n_head, sub_rows, group_heads, HD) for tensor in relaid])
    packed = jnp.einsum(
        "hltcr,xlthd->xhclrd", home_table, stacked, preferred_element_type=jnp.float32
    ).astype(jnp.bfloat16)
    packed = packed.reshape(3, per_owner, n_seq, lane_count, HD)
    markers = (
        jnp.sum(home_table.astype(jnp.float32), axis=2).transpose(0, 2, 1, 3).astype(jnp.bfloat16)
    )
    markers = markers.reshape(1, per_owner, n_seq, lane_count)
    returned = attend_and_return(
        (
            lax.all_to_all(packed, "seq", split_axis=2, concat_axis=2, tiled=True),
            lax.all_to_all(markers, "seq", split_axis=2, concat_axis=2, tiled=True),
        )
    )
    returned = returned.reshape(group_heads, CLUSTERS, n_head, slot_depth, HD)
    gathered = jnp.einsum(
        "hltcr,hclrd->lthd", home_table, returned, preferred_element_type=jnp.float32
    ).astype(jnp.bfloat16)
    gathered = gathered.reshape(tok_dev, group_heads * HD)
    partial_value = jnp.dot(
        gathered,
        lax.all_gather(out_weight, "seq", axis=1, tiled=True),
        preferred_element_type=jnp.float32,
    )
    return lax.psum_scatter(
        partial_value.astype(jnp.bfloat16), "head", scatter_dimension=1, tiled=True
    )


def head_slots(block_ids, most):
    onehot = block_ids[:, None, :] == jnp.arange(CLUSTERS, dtype=jnp.int32)[None, :, None]
    rows = block_ids.shape[-1]
    before = (jnp.arange(rows)[:, None] < jnp.arange(rows)[None, :]).astype(jnp.bfloat16)
    running = jnp.einsum("bcs,st->bct", onehot.astype(jnp.bfloat16), before, preferred_element_type=jnp.float32)
    depth = jnp.arange(most, dtype=jnp.float32)
    hit = onehot[:, :, None, :] & (running[:, :, None, :] == depth[None, None, :, None])
    return hit.astype(jnp.bfloat16)


def head_body(queries, keys, values, cluster_ids, out_weight):
    n_seq = lax.axis_size("seq")
    n_head = lax.axis_size("head")
    n_dev = n_seq * n_head
    tok_dev = cluster_ids.shape[1]
    sub_rows = tok_dev // n_head
    group_heads = HEADS // n_head
    most = max(2, 2 * tok_dev // (n_head * CLUSTERS))
    head_group = lax.axis_index("head")
    group_ids = lax.dynamic_slice_in_dim(cluster_ids[:, :, 0], head_group * group_heads, group_heads, 0)
    ids = lax.all_to_all(group_ids, "seq", split_axis=0, concat_axis=0, tiled=True)
    ids = ids.reshape(n_seq * n_head, sub_rows)

    def route(tensor):
        split = tensor.reshape(sub_rows, n_dev, HD).transpose(1, 0, 2)
        moved = lax.all_to_all(split, ("head", "seq"), split_axis=0, concat_axis=0, tiled=True)
        return moved.reshape(n_head, n_seq, sub_rows, HD).transpose(1, 0, 2, 3).reshape(n_dev, sub_rows, HD)

    table = head_slots(ids, most)
    stacked = jnp.stack([route(queries), route(keys), route(values)])
    packed = jnp.einsum(
        "bcrt,xbtd->xcbrd", table, stacked, preferred_element_type=jnp.float32
    ).astype(jnp.bfloat16)
    packed = packed.reshape(3, CLUSTERS, n_dev * most, HD)
    markers = jnp.sum(table.astype(jnp.float32), axis=3).transpose(1, 0, 2).reshape(CLUSTERS, n_dev * most)
    result = attend_blocks(packed, markers).reshape(CLUSTERS, n_dev, most, HD)
    back = jnp.einsum(
        "bcrt,cbrd->btd", table, result, preferred_element_type=jnp.float32
    ).astype(jnp.bfloat16)
    back = back.reshape(n_seq, tok_dev, HD)
    gathered = lax.all_to_all(back, "seq", split_axis=0, concat_axis=0, tiled=True)
    gathered = gathered.transpose(1, 0, 2).reshape(tok_dev, group_heads * HD)
    partial_value = jnp.dot(
        gathered,
        lax.all_gather(out_weight, "seq", axis=1, tiled=True),
        preferred_element_type=jnp.float32,
    )
    return lax.psum_scatter(
        partial_value.astype(jnp.bfloat16), "head", scatter_dimension=1, tiled=True
    )


def solution(mesh):
    in_specs = (
        P(("seq", "head"), None),
        P(("seq", "head"), None),
        P(("seq", "head"), None),
        P(None, "seq", None),
        P("head", "seq"),
    )
    out_specs = P("seq", "head")
    body = head_body if mesh.size == HEADS else generic_body
    return jax.shard_map(body, mesh=mesh, in_specs=in_specs, out_specs=out_specs, check_vma=False)
```

```python
import functools

import jax
import jax.numpy as jnp
from jax import lax
from jax.experimental import pallas as pl
from jax.experimental.pallas import tpu as pltpu
from jax.sharding import PartitionSpec as P

HEADS = 32
HD = 128
CLUSTERS = 128


def slot_table(block_ids, slot_depth):
    sub_rows = block_ids.shape[-1]
    onehot = (block_ids[..., None] == jnp.arange(CLUSTERS, dtype=jnp.int32)).astype(jnp.float32)
    lower = (jnp.arange(sub_rows)[:, None] >= jnp.arange(sub_rows)[None, :]).astype(jnp.float32)
    running = jnp.einsum("ts,abse->abte", lower, onehot)
    ranking = (jnp.sum(running * onehot, axis=-1) - 1.0).astype(jnp.int32)
    depth_hit = (ranking[..., None] == jnp.arange(slot_depth, dtype=jnp.int32)).astype(jnp.bfloat16)
    return onehot.astype(jnp.bfloat16)[..., :, None] * depth_hit[..., None, :]


def attend_blocks(packed, validity):
    scores = jnp.einsum(
        "cqd,ckd->cqk", packed[0], packed[1], preferred_element_type=jnp.float32
    ) * HD ** (-0.5)
    scores = jnp.where(validity[:, None, :] > 0, scores, -1e30)
    row_max = jnp.max(scores, axis=-1, keepdims=True)
    raised = jnp.exp(scores - row_max)
    weights = (raised / jnp.sum(raised, axis=-1, keepdims=True)).astype(jnp.bfloat16)
    return jnp.einsum(
        "cqk,ckd->cqd", weights, packed[2], preferred_element_type=jnp.float32
    ).astype(jnp.bfloat16)


def attend_and_return(arrived):
    packed, markers = arrived
    item_count = packed.shape[1]
    n_seq = packed.shape[2]
    lane_count = packed.shape[3]
    result_block = attend_blocks(
        packed.reshape(3, item_count, n_seq * lane_count, HD),
        markers.reshape(item_count, n_seq * lane_count),
    )
    result_block = result_block.reshape(item_count, n_seq, lane_count, HD)
    return lax.all_to_all(result_block, "seq", split_axis=1, concat_axis=1, tiled=True)


def generic_body(queries, keys, values, cluster_ids, out_weight):
    n_seq = lax.axis_size("seq")
    n_head = lax.axis_size("head")
    head_group = lax.axis_index("head")
    tok_dev = cluster_ids.shape[1]
    sub_rows = tok_dev // n_head
    group_heads = HEADS // n_head
    slot_depth = max(2, 2 * tok_dev // (n_head * CLUSTERS))
    lane_count = n_head * slot_depth
    per_owner = group_heads * CLUSTERS // n_seq
    all_ids = cluster_ids[:, :, 0]
    group_ids = lax.dynamic_slice_in_dim(all_ids, head_group * group_heads, group_heads, 0)
    group_ids = group_ids.reshape(group_heads, n_head, sub_rows)
    home_table = slot_table(group_ids, slot_depth)
    relaid = (
        lax.all_to_all(queries, "head", split_axis=1, concat_axis=0, tiled=True),
        lax.all_to_all(keys, "head", split_axis=1, concat_axis=0, tiled=True),
        lax.all_to_all(values, "head", split_axis=1, concat_axis=0, tiled=True),
    )
    stacked = jnp.stack([tensor.reshape(n_head, sub_rows, group_heads, HD) for tensor in relaid])
    packed = jnp.einsum(
        "hltcr,xlthd->xhclrd", home_table, stacked, preferred_element_type=jnp.float32
    ).astype(jnp.bfloat16)
    packed = packed.reshape(3, per_owner, n_seq, lane_count, HD)
    markers = (
        jnp.sum(home_table.astype(jnp.float32), axis=2).transpose(0, 2, 1, 3).astype(jnp.bfloat16)
    )
    markers = markers.reshape(1, per_owner, n_seq, lane_count)
    returned = attend_and_return(
        (
            lax.all_to_all(packed, "seq", split_axis=2, concat_axis=2, tiled=True),
            lax.all_to_all(markers, "seq", split_axis=2, concat_axis=2, tiled=True),
        )
    )
    returned = returned.reshape(group_heads, CLUSTERS, n_head, slot_depth, HD)
    gathered = jnp.einsum(
        "hltcr,hclrd->lthd", home_table, returned, preferred_element_type=jnp.float32
    ).astype(jnp.bfloat16)
    gathered = gathered.reshape(tok_dev, group_heads * HD)
    partial_value = jnp.dot(
        gathered,
        lax.all_gather(out_weight, "seq", axis=1, tiled=True),
        preferred_element_type=jnp.float32,
    )
    return lax.psum_scatter(
        partial_value.astype(jnp.bfloat16), "head", scatter_dimension=1, tiled=True
    )


GROUP = 16
CHUNK = 16


def flipped(index, mask, count):
    total, bit = 0, 1
    while bit < count:
        total = total + (index // bit + mask // bit) % 2 * bit
        bit *= 2
    return total


def attend_kernel(
    n_seq, n_head, most,
    q_ref, k_ref, v_ref, code_ref, att_ref,
    recv, rcode, packed, marks, result, back,
    out_sem, in_sem, code_out, code_in, back_out, back_in,
):
    n_dev = n_seq * n_head
    per_group = GROUP // most
    n_group = n_dev // per_group
    sub = q_ref.shape[0]
    tok = n_head * sub
    wide = per_group * sub
    me_s, me_x = lax.axis_index("seq"), lax.axis_index("head")
    me = me_x * n_seq + me_s
    block = me_s * n_head + me_x
    my_group = block // per_group
    slots = CLUSTERS * GROUP

    def place(index):
        return {"seq": index % n_seq, "head": index // n_seq}

    def group_mask(step):
        return step % 2 * (n_group // 2) + step // 2

    def landing(source, part):
        rows = pl.ds(pl.multiple_of(source % per_group * sub, sub), sub)
        return recv.at[source // per_group, rows, part * HD:(part + 1) * HD]

    def code_landing(source):
        lanes = pl.ds(pl.multiple_of(source % per_group * sub, sub), sub)
        return rcode.at[source // per_group, :, lanes]

    def columns(index):
        return pl.ds(pl.multiple_of(index * HD, HD), HD)

    parts = (q_ref, k_ref, v_ref)

    barrier = pltpu.get_barrier_semaphore()

    def greet(step, carry):
        pl.semaphore_signal(
            barrier, inc=1, device_id=place((me + step) % n_dev), device_id_type=pl.DeviceIdType.MESH
        )
        return carry

    for part, ref in enumerate(parts):
        pltpu.make_async_copy(ref.at[:, columns(me)], landing(block, part), in_sem.at[part, block]).start()
    pltpu.make_async_copy(code_ref.at[me], code_landing(block), code_in.at[block]).start()
    lax.fori_loop(1, n_dev, greet, 0)
    pl.semaphore_wait(barrier, n_dev - 1)

    def target(step):
        inner = step % 4
        mask = group_mask(step // 4) * 2 + inner % 2 + inner // 2 * n_seq
        return flipped(me, mask, n_dev)

    def code_copy(dst):
        return pltpu.make_async_remote_copy(
            src_ref=code_ref.at[dst], dst_ref=code_landing(block),
            send_sem=code_out.at[dst], recv_sem=code_in.at[block],
            device_id=place(dst), device_id_type=pl.DeviceIdType.MESH,
        )

    def row_copy(dst, part):
        return pltpu.make_async_remote_copy(
            src_ref=parts[part].at[:, columns(dst)], dst_ref=landing(block, part),
            send_sem=out_sem.at[part, dst], recv_sem=in_sem.at[part, block],
            device_id=place(dst), device_id_type=pl.DeviceIdType.MESH,
        )

    def send(step, carry):
        dst = target(step)
        code_copy(dst).start()
        for part in range(3):
            row_copy(dst, part).start()
        return carry

    lax.fori_loop(1, n_dev, send, 0)

    ones = jnp.ones((wide, HD), jnp.bfloat16)

    def pack_group(step, carry):
        group = flipped(my_group, group_mask(step), n_group)

        def arrive(inner, carry):
            source = group * per_group + inner
            pltpu.make_async_copy(code_landing(source), code_landing(source), code_in.at[source]).wait()
            for part in range(3):
                pltpu.make_async_copy(landing(source, part), landing(source, part), in_sem.at[part, source]).wait()
            return carry

        lax.fori_loop(0, per_group, arrive, 0)

        def pack_chunk(chunk, carry):
            rows = lax.broadcasted_iota(jnp.int32, (CHUNK * GROUP, wide), 0) + chunk * (CHUNK * GROUP)
            hit = jnp.where(rcode[group] == rows, 1.0, 0.0).astype(jnp.bfloat16)
            at = (
                pl.ds(chunk * CHUNK, CHUNK),
                pl.ds(pl.multiple_of(group * GROUP, GROUP), GROUP),
            )
            data = jnp.dot(hit, recv[group], preferred_element_type=jnp.float32).astype(jnp.bfloat16)
            packed[at[0], at[1], :] = data.reshape(CHUNK, GROUP, 3 * HD)
            mark = jnp.dot(hit, ones, preferred_element_type=jnp.float32).astype(jnp.bfloat16)
            marks[at[0], at[1], :] = mark.reshape(CHUNK, GROUP, HD)
            return carry

        return lax.fori_loop(0, CLUSTERS // CHUNK, pack_chunk, carry)

    lax.fori_loop(0, n_group, pack_group, 0)

    def attend(step, carry):
        for inner in range(4):
            cluster = step * 4 + inner
            scores = lax.dot_general(
                packed[cluster, :, HD:2 * HD], packed[cluster, :, 0:HD],
                (((1,), (1,)), ((), ())), preferred_element_type=jnp.float32,
            ) * HD ** (-0.5)
            scores = jnp.where(marks[cluster].astype(jnp.float32) > 0, scores, -1e30)
            raised = jnp.exp(scores - jnp.max(scores, axis=0, keepdims=True))
            weights = (raised / jnp.sum(raised, axis=0, keepdims=True)).astype(jnp.bfloat16)
            result[cluster] = lax.dot_general(
                weights, packed[cluster, :, 2 * HD:3 * HD],
                (((0,), (0,)), ((), ())), preferred_element_type=jnp.float32,
            ).astype(jnp.bfloat16)
        return carry

    lax.fori_loop(0, CLUSTERS // 4, attend, 0)

    seqs = per_group // n_head

    def back_copy(group, part):
        dst = group * seqs + part
        return pltpu.make_async_remote_copy(
            src_ref=back.at[group, part * tok:(part + 1) * tok, :], dst_ref=att_ref.at[:, columns(me_s)],
            send_sem=back_out.at[dst], recv_sem=back_in.at[me_s],
            device_id={"seq": dst, "head": me_x}, device_id_type=pl.DeviceIdType.MESH,
        )

    def unpack(group):
        rows = result[:, pl.ds(pl.multiple_of(group * GROUP, GROUP), GROUP), :].reshape(slots, HD)
        for part in range(seqs):
            lanes = slice(part * tok, (part + 1) * tok)
            hit = rcode[group, :, lanes] == lax.broadcasted_iota(jnp.int32, (slots, tok), 0)
            hit = jnp.where(hit, 1.0, 0.0).astype(jnp.bfloat16)
            turned = lax.dot_general(
                rows, hit, (((0,), (0,)), ((), ())), preferred_element_type=jnp.float32
            )
            back[group, lanes, :] = turned.T.astype(jnp.bfloat16)

    def send_back(step, carry):
        group = flipped(my_group, group_mask(n_group - step), n_group)
        unpack(group)
        for part in range(seqs):
            back_copy(group, part).start()
        return carry

    lax.fori_loop(1, n_group, send_back, 0)
    unpack(my_group)
    own = me_s % seqs
    own_rows = pl.ds(pl.multiple_of(own * tok, tok), tok)
    local = pltpu.make_async_copy(back.at[my_group, own_rows, :], att_ref.at[:, columns(me_s)], back_in.at[me_s])
    local.start()

    def send_near(step, carry):
        part = (own + step) % seqs
        dst = my_group * seqs + part
        pltpu.make_async_remote_copy(
            src_ref=back.at[my_group, pl.ds(pl.multiple_of(part * tok, tok), tok), :],
            dst_ref=att_ref.at[:, columns(me_s)],
            send_sem=back_out.at[dst], recv_sem=back_in.at[me_s],
            device_id={"seq": dst, "head": me_x}, device_id_type=pl.DeviceIdType.MESH,
        ).start()
        return carry

    lax.fori_loop(1, seqs, send_near, 0)

    def finish_sends(step, carry):
        dst = target(step)
        code_copy(dst).wait_send()
        for part in range(3):
            row_copy(dst, part).wait_send()
        return carry

    lax.fori_loop(1, n_dev, finish_sends, 0)
    local.wait()

    def finish_back(step, carry):
        other = (me_s + step) % n_seq
        landed = att_ref.at[:, columns(other)]
        pltpu.make_async_copy(landed, landed, back_in.at[other]).wait()
        left = back.at[other // seqs, pl.ds(pl.multiple_of(other % seqs * tok, tok), tok), :]
        pltpu.make_async_copy(left, left, back_out.at[other]).wait()
        return carry

    lax.fori_loop(1, n_seq, finish_back, 0)


def head_body(queries, keys, values, cluster_ids, out_weight):
    n_seq = lax.axis_size("seq")
    n_head = lax.axis_size("head")
    n_dev = n_seq * n_head
    tok_dev = cluster_ids.shape[1]
    sub_rows = tok_dev // n_head
    group_heads = HEADS // n_head
    most = max(2, 2 * tok_dev // (n_head * CLUSTERS))
    per_group = GROUP // most
    n_group = n_dev // per_group
    wide = per_group * sub_rows
    head_group = lax.axis_index("head")
    block = lax.axis_index("seq") * n_head + head_group
    ids = lax.dynamic_slice_in_dim(cluster_ids[:, :, 0], head_group * sub_rows, sub_rows, 1)
    earlier = jnp.arange(sub_rows)[:, None] < jnp.arange(sub_rows)[None, :]
    same = (ids[:, :, None] == ids[:, None, :]) & earlier[None]
    ranking = jnp.sum(same.astype(jnp.int32), axis=1)
    codes = ids * GROUP + (block % per_group) * most + ranking
    codes = codes.reshape(HEADS, 1, sub_rows)
    anywhere = pl.BlockSpec(memory_space=pl.ANY)
    attended = pl.pallas_call(
        functools.partial(attend_kernel, n_seq, n_head, most),
        out_shape=jax.ShapeDtypeStruct((tok_dev, group_heads * HD), jnp.bfloat16),
        in_specs=[anywhere, anywhere, anywhere, pl.BlockSpec(memory_space=pltpu.VMEM)],
        out_specs=anywhere,
        scratch_shapes=[
            pltpu.VMEM((n_group, wide, 3 * HD), jnp.bfloat16),
            pltpu.VMEM((n_group, 1, wide), jnp.int32),
            pltpu.VMEM((CLUSTERS, n_group * GROUP, 3 * HD), jnp.bfloat16),
            pltpu.VMEM((CLUSTERS, n_group * GROUP, HD), jnp.bfloat16),
            pltpu.VMEM((CLUSTERS, n_group * GROUP, HD), jnp.bfloat16),
            pltpu.VMEM((n_group, wide, HD), jnp.bfloat16),
            pltpu.SemaphoreType.DMA((3, n_dev)),
            pltpu.SemaphoreType.DMA((3, n_dev)),
            pltpu.SemaphoreType.DMA((n_dev,)),
            pltpu.SemaphoreType.DMA((n_dev,)),
            pltpu.SemaphoreType.DMA((n_seq,)),
            pltpu.SemaphoreType.DMA((n_seq,)),
        ],
        compiler_params=pltpu.CompilerParams(
            collective_id=0, has_side_effects=True, vmem_limit_bytes=56 * 2 ** 20
        ),
        cost_estimate=pl.CostEstimate(flops=2 * 10 ** 10, bytes_accessed=2 * 10 ** 7, transcendentals=2 ** 21),
    )(queries, keys, values, codes)
    partial_value = jnp.dot(
        attended,
        lax.all_gather(out_weight, "seq", axis=1, tiled=True),
        preferred_element_type=jnp.float32,
    )
    return lax.psum_scatter(
        partial_value.astype(jnp.bfloat16), "head", scatter_dimension=1, tiled=True
    )


def solution(mesh):
    in_specs = (
        P(("seq", "head"), None),
        P(("seq", "head"), None),
        P(("seq", "head"), None),
        P(None, "seq", None),
        P("head", "seq"),
    )
    out_specs = P("seq", "head")
    body = head_body if mesh.size == HEADS and mesh.shape["head"] == 2 else generic_body
    return jax.shard_map(body, mesh=mesh, in_specs=in_specs, out_specs=out_specs, check_vma=False)
```

```python
import functools

import jax
import jax.numpy as jnp
from jax import lax
from jax.experimental import pallas as pl
from jax.experimental.pallas import tpu as pltpu
from jax.sharding import PartitionSpec as P

HEADS = 32
HD = 128
CLUSTERS = 128


def slot_table(block_ids, slot_depth):
    sub_rows = block_ids.shape[-1]
    onehot = (block_ids[..., None] == jnp.arange(CLUSTERS, dtype=jnp.int32)).astype(jnp.float32)
    lower = (jnp.arange(sub_rows)[:, None] >= jnp.arange(sub_rows)[None, :]).astype(jnp.float32)
    running = jnp.einsum("ts,abse->abte", lower, onehot)
    ranking = (jnp.sum(running * onehot, axis=-1) - 1.0).astype(jnp.int32)
    depth_hit = (ranking[..., None] == jnp.arange(slot_depth, dtype=jnp.int32)).astype(jnp.bfloat16)
    return onehot.astype(jnp.bfloat16)[..., :, None] * depth_hit[..., None, :]


def attend_blocks(packed, validity):
    scores = jnp.einsum(
        "cqd,ckd->cqk", packed[0], packed[1], preferred_element_type=jnp.float32
    ) * HD ** (-0.5)
    scores = jnp.where(validity[:, None, :] > 0, scores, -1e30)
    row_max = jnp.max(scores, axis=-1, keepdims=True)
    raised = jnp.exp(scores - row_max)
    weights = (raised / jnp.sum(raised, axis=-1, keepdims=True)).astype(jnp.bfloat16)
    return jnp.einsum(
        "cqk,ckd->cqd", weights, packed[2], preferred_element_type=jnp.float32
    ).astype(jnp.bfloat16)


def attend_and_return(arrived):
    packed, markers = arrived
    item_count = packed.shape[1]
    n_seq = packed.shape[2]
    lane_count = packed.shape[3]
    result_block = attend_blocks(
        packed.reshape(3, item_count, n_seq * lane_count, HD),
        markers.reshape(item_count, n_seq * lane_count),
    )
    result_block = result_block.reshape(item_count, n_seq, lane_count, HD)
    return lax.all_to_all(result_block, "seq", split_axis=1, concat_axis=1, tiled=True)


def generic_body(queries, keys, values, cluster_ids, out_weight):
    n_seq = lax.axis_size("seq")
    n_head = lax.axis_size("head")
    head_group = lax.axis_index("head")
    tok_dev = cluster_ids.shape[1]
    sub_rows = tok_dev // n_head
    group_heads = HEADS // n_head
    slot_depth = max(2, 2 * tok_dev // (n_head * CLUSTERS))
    lane_count = n_head * slot_depth
    per_owner = group_heads * CLUSTERS // n_seq
    all_ids = cluster_ids[:, :, 0]
    group_ids = lax.dynamic_slice_in_dim(all_ids, head_group * group_heads, group_heads, 0)
    group_ids = group_ids.reshape(group_heads, n_head, sub_rows)
    home_table = slot_table(group_ids, slot_depth)
    relaid = (
        lax.all_to_all(queries, "head", split_axis=1, concat_axis=0, tiled=True),
        lax.all_to_all(keys, "head", split_axis=1, concat_axis=0, tiled=True),
        lax.all_to_all(values, "head", split_axis=1, concat_axis=0, tiled=True),
    )
    stacked = jnp.stack([tensor.reshape(n_head, sub_rows, group_heads, HD) for tensor in relaid])
    packed = jnp.einsum(
        "hltcr,xlthd->xhclrd", home_table, stacked, preferred_element_type=jnp.float32
    ).astype(jnp.bfloat16)
    packed = packed.reshape(3, per_owner, n_seq, lane_count, HD)
    markers = (
        jnp.sum(home_table.astype(jnp.float32), axis=2).transpose(0, 2, 1, 3).astype(jnp.bfloat16)
    )
    markers = markers.reshape(1, per_owner, n_seq, lane_count)
    returned = attend_and_return(
        (
            lax.all_to_all(packed, "seq", split_axis=2, concat_axis=2, tiled=True),
            lax.all_to_all(markers, "seq", split_axis=2, concat_axis=2, tiled=True),
        )
    )
    returned = returned.reshape(group_heads, CLUSTERS, n_head, slot_depth, HD)
    gathered = jnp.einsum(
        "hltcr,hclrd->lthd", home_table, returned, preferred_element_type=jnp.float32
    ).astype(jnp.bfloat16)
    gathered = gathered.reshape(tok_dev, group_heads * HD)
    partial_value = jnp.dot(
        gathered,
        lax.all_gather(out_weight, "seq", axis=1, tiled=True),
        preferred_element_type=jnp.float32,
    )
    return lax.psum_scatter(
        partial_value.astype(jnp.bfloat16), "head", scatter_dimension=1, tiled=True
    )


GROUP = 16
CHUNK = 16


def flipped(index, mask, count):
    total, bit = 0, 1
    while bit < count:
        total = total + (index // bit + mask // bit) % 2 * bit
        bit *= 2
    return total


def attend_kernel(
    n_seq, n_head, most,
    q_ref, k_ref, v_ref, w_ref, code_ref, att_ref, whole_ref,
    recv, rcode, packed, marks, result, back,
    out_sem, in_sem, code_out, code_in, back_out, back_in, weight_out, weight_in,
):
    n_dev = n_seq * n_head
    per_group = GROUP // most
    n_group = n_dev // per_group
    sub = q_ref.shape[0]
    tok = n_head * sub
    wide = per_group * sub
    me_s, me_x = lax.axis_index("seq"), lax.axis_index("head")
    me = me_x * n_seq + me_s
    block = me_s * n_head + me_x
    my_group = block // per_group
    slots = CLUSTERS * GROUP

    def place(index):
        return {"seq": index % n_seq, "head": index // n_seq}

    def group_mask(step):
        return step % 2 * (n_group // 2) + step // 2

    def landing(source, part):
        rows = pl.ds(pl.multiple_of(source % per_group * sub, sub), sub)
        return recv.at[source // per_group, rows, part * HD:(part + 1) * HD]

    def code_landing(source):
        lanes = pl.ds(pl.multiple_of(source % per_group * sub, sub), sub)
        return rcode.at[source // per_group, :, lanes]

    def columns(index):
        return pl.ds(pl.multiple_of(index * HD, HD), HD)

    parts = (q_ref, k_ref, v_ref)

    barrier = pltpu.get_barrier_semaphore()

    def greet(step, carry):
        pl.semaphore_signal(
            barrier, inc=1, device_id=place((me + step) % n_dev), device_id_type=pl.DeviceIdType.MESH
        )
        return carry

    for part, ref in enumerate(parts):
        pltpu.make_async_copy(ref.at[:, columns(me)], landing(block, part), in_sem.at[part, block]).start()
    pltpu.make_async_copy(code_ref.at[me], code_landing(block), code_in.at[block]).start()
    lax.fori_loop(1, n_dev, greet, 0)
    pl.semaphore_wait(barrier, n_dev - 1)

    def target(step):
        inner = step % 4
        mask = group_mask(step // 4) * 2 + inner % 2 + inner // 2 * n_seq
        return flipped(me, mask, n_dev)

    def code_copy(dst):
        return pltpu.make_async_remote_copy(
            src_ref=code_ref.at[dst], dst_ref=code_landing(block),
            send_sem=code_out.at[dst], recv_sem=code_in.at[block],
            device_id=place(dst), device_id_type=pl.DeviceIdType.MESH,
        )

    def row_copy(dst, part):
        return pltpu.make_async_remote_copy(
            src_ref=parts[part].at[:, columns(dst)], dst_ref=landing(block, part),
            send_sem=out_sem.at[part, dst], recv_sem=in_sem.at[part, block],
            device_id=place(dst), device_id_type=pl.DeviceIdType.MESH,
        )

    def send(step, carry):
        dst = target(step)
        code_copy(dst).start()
        for part in range(3):
            row_copy(dst, part).start()
        return carry

    width = w_ref.shape[1]

    def weight_block(index):
        return whole_ref.at[:, pl.ds(pl.multiple_of(index * width, width), width)]

    def weight_copy(stage, item):
        mask = n_seq >> (stage + 1)
        held = flipped(me_s, item * (2 * mask), n_seq)
        return pltpu.make_async_remote_copy(
            src_ref=w_ref if stage == 0 else weight_block(held), dst_ref=weight_block(held),
            send_sem=weight_out.at[2 ** stage - 1 + item], recv_sem=weight_in.at[held],
            device_id={"seq": flipped(me_s, mask, n_seq), "head": me_x},
            device_id_type=pl.DeviceIdType.MESH,
        )

    stages = n_seq.bit_length() - 1

    def spread(stage):
        if stage > 0:
            weights_arrive(stage - 1)
        for item in range(2 ** stage):
            weight_copy(stage, item).start()

    def weights_arrive(stage):
        mask = n_seq >> (stage + 1)
        for item in range(2 ** stage):
            new = flipped(me_s, item * (2 * mask) + mask, n_seq)
            pltpu.make_async_copy(weight_block(new), weight_block(new), weight_in.at[new]).wait()

    own_weight = pltpu.make_async_copy(w_ref, weight_block(me_s), weight_in.at[me_s])
    own_weight.start()
    spread(0)
    lax.fori_loop(1, n_dev, send, 0)
    own_weight.wait()

    ones = jnp.ones((wide, HD), jnp.bfloat16)

    def pack_group(step, carry):
        group = flipped(my_group, group_mask(step), n_group)

        def arrive(inner, carry):
            source = group * per_group + inner
            pltpu.make_async_copy(code_landing(source), code_landing(source), code_in.at[source]).wait()
            for part in range(3):
                pltpu.make_async_copy(landing(source, part), landing(source, part), in_sem.at[part, source]).wait()
            return carry

        lax.fori_loop(0, per_group, arrive, 0)

        def pack_chunk(chunk, carry):
            rows = lax.broadcasted_iota(jnp.int32, (CHUNK * GROUP, wide), 0) + chunk * (CHUNK * GROUP)
            hit = jnp.where(rcode[group] == rows, 1.0, 0.0).astype(jnp.bfloat16)
            at = (
                pl.ds(chunk * CHUNK, CHUNK),
                pl.ds(pl.multiple_of(group * GROUP, GROUP), GROUP),
            )
            data = jnp.dot(hit, recv[group], preferred_element_type=jnp.float32).astype(jnp.bfloat16)
            packed[at[0], at[1], :] = data.reshape(CHUNK, GROUP, 3 * HD)
            mark = jnp.dot(hit, ones, preferred_element_type=jnp.float32).astype(jnp.bfloat16)
            marks[at[0], at[1], :] = mark.reshape(CHUNK, GROUP, HD)
            return carry

        return lax.fori_loop(0, CLUSTERS // CHUNK, pack_chunk, carry)

    lax.fori_loop(0, 2, pack_group, 0)
    spread(1)
    lax.fori_loop(2, 4, pack_group, 0)
    spread(2)
    lax.fori_loop(4, n_group, pack_group, 0)

    def attend(step, carry):
        for inner in range(4):
            cluster = step * 4 + inner
            scores = lax.dot_general(
                packed[cluster, :, HD:2 * HD], packed[cluster, :, 0:HD],
                (((1,), (1,)), ((), ())), preferred_element_type=jnp.float32,
            ) * HD ** (-0.5)
            scores = jnp.where(marks[cluster].astype(jnp.float32) > 0, scores, -1e30)
            raised = jnp.exp(scores - jnp.max(scores, axis=0, keepdims=True))
            weights = (raised / jnp.sum(raised, axis=0, keepdims=True)).astype(jnp.bfloat16)
            result[cluster] = lax.dot_general(
                weights, packed[cluster, :, 2 * HD:3 * HD],
                (((0,), (0,)), ((), ())), preferred_element_type=jnp.float32,
            ).astype(jnp.bfloat16)
        return carry

    lax.fori_loop(0, CLUSTERS // 4, attend, 0)

    seqs = per_group // n_head

    def back_copy(group, part):
        dst = group * seqs + part
        return pltpu.make_async_remote_copy(
            src_ref=back.at[group, part * tok:(part + 1) * tok, :], dst_ref=att_ref.at[:, columns(me_s)],
            send_sem=back_out.at[dst], recv_sem=back_in.at[me_s],
            device_id={"seq": dst, "head": me_x}, device_id_type=pl.DeviceIdType.MESH,
        )

    def unpack(group):
        rows = result[:, pl.ds(pl.multiple_of(group * GROUP, GROUP), GROUP), :].reshape(slots, HD)
        for part in range(seqs):
            lanes = slice(part * tok, (part + 1) * tok)
            hit = rcode[group, :, lanes] == lax.broadcasted_iota(jnp.int32, (slots, tok), 0)
            hit = jnp.where(hit, 1.0, 0.0).astype(jnp.bfloat16)
            turned = lax.dot_general(
                rows, hit, (((0,), (0,)), ((), ())), preferred_element_type=jnp.float32
            )
            back[group, lanes, :] = turned.T.astype(jnp.bfloat16)

    def send_back(step, carry):
        group = flipped(my_group, group_mask(n_group - step), n_group)
        unpack(group)
        for part in range(seqs):
            back_copy(group, part).start()
        return carry

    lax.fori_loop(1, n_group, send_back, 0)
    unpack(my_group)
    spread(3)
    own = me_s % seqs
    own_rows = pl.ds(pl.multiple_of(own * tok, tok), tok)
    local = pltpu.make_async_copy(back.at[my_group, own_rows, :], att_ref.at[:, columns(me_s)], back_in.at[me_s])
    local.start()

    def send_near(step, carry):
        part = (own + step) % seqs
        dst = my_group * seqs + part
        pltpu.make_async_remote_copy(
            src_ref=back.at[my_group, pl.ds(pl.multiple_of(part * tok, tok), tok), :],
            dst_ref=att_ref.at[:, columns(me_s)],
            send_sem=back_out.at[dst], recv_sem=back_in.at[me_s],
            device_id={"seq": dst, "head": me_x}, device_id_type=pl.DeviceIdType.MESH,
        ).start()
        return carry

    lax.fori_loop(1, seqs, send_near, 0)

    def finish_sends(step, carry):
        dst = target(step)
        code_copy(dst).wait_send()
        for part in range(3):
            row_copy(dst, part).wait_send()
        return carry

    lax.fori_loop(1, n_dev, finish_sends, 0)
    local.wait()

    def finish_back(step, carry):
        other = (me_s + step) % n_seq
        landed = att_ref.at[:, columns(other)]
        pltpu.make_async_copy(landed, landed, back_in.at[other]).wait()
        left = back.at[other // seqs, pl.ds(pl.multiple_of(other % seqs * tok, tok), tok), :]
        pltpu.make_async_copy(left, left, back_out.at[other]).wait()
        return carry

    lax.fori_loop(1, n_seq, finish_back, 0)
    weights_arrive(stages - 1)
    for stage in range(stages):
        for item in range(2 ** stage):
            weight_copy(stage, item).wait_send()


def head_body(queries, keys, values, cluster_ids, out_weight):
    n_seq = lax.axis_size("seq")
    n_head = lax.axis_size("head")
    n_dev = n_seq * n_head
    tok_dev = cluster_ids.shape[1]
    sub_rows = tok_dev // n_head
    group_heads = HEADS // n_head
    most = max(2, 2 * tok_dev // (n_head * CLUSTERS))
    per_group = GROUP // most
    n_group = n_dev // per_group
    wide = per_group * sub_rows
    head_group = lax.axis_index("head")
    block = lax.axis_index("seq") * n_head + head_group
    ids = lax.dynamic_slice_in_dim(cluster_ids[:, :, 0], head_group * sub_rows, sub_rows, 1)
    earlier = jnp.arange(sub_rows)[:, None] < jnp.arange(sub_rows)[None, :]
    same = (ids[:, :, None] == ids[:, None, :]) & earlier[None]
    ranking = jnp.sum(same.astype(jnp.int32), axis=1)
    codes = ids * GROUP + (block % per_group) * most + ranking
    codes = codes.reshape(HEADS, 1, sub_rows)
    anywhere = pl.BlockSpec(memory_space=pl.ANY)
    attended, whole = pl.pallas_call(
        functools.partial(attend_kernel, n_seq, n_head, most),
        out_shape=(
            jax.ShapeDtypeStruct((tok_dev, group_heads * HD), jnp.bfloat16),
            jax.ShapeDtypeStruct((out_weight.shape[0], n_seq * out_weight.shape[1]), jnp.bfloat16),
        ),
        in_specs=[anywhere, anywhere, anywhere, anywhere, pl.BlockSpec(memory_space=pltpu.VMEM)],
        out_specs=(anywhere, anywhere),
        scratch_shapes=[
            pltpu.VMEM((n_group, wide, 3 * HD), jnp.bfloat16),
            pltpu.VMEM((n_group, 1, wide), jnp.int32),
            pltpu.VMEM((CLUSTERS, n_group * GROUP, 3 * HD), jnp.bfloat16),
            pltpu.VMEM((CLUSTERS, n_group * GROUP, HD), jnp.bfloat16),
            pltpu.VMEM((CLUSTERS, n_group * GROUP, HD), jnp.bfloat16),
            pltpu.VMEM((n_group, wide, HD), jnp.bfloat16),
            pltpu.SemaphoreType.DMA((3, n_dev)),
            pltpu.SemaphoreType.DMA((3, n_dev)),
            pltpu.SemaphoreType.DMA((n_dev,)),
            pltpu.SemaphoreType.DMA((n_dev,)),
            pltpu.SemaphoreType.DMA((n_seq,)),
            pltpu.SemaphoreType.DMA((n_seq,)),
            pltpu.SemaphoreType.DMA((n_seq,)),
            pltpu.SemaphoreType.DMA((n_seq,)),
        ],
        compiler_params=pltpu.CompilerParams(
            collective_id=0, has_side_effects=True, vmem_limit_bytes=56 * 2 ** 20
        ),
        cost_estimate=pl.CostEstimate(flops=2 * 10 ** 10, bytes_accessed=2 * 10 ** 7, transcendentals=2 ** 21),
    )(queries, keys, values, out_weight, codes)
    half = whole.shape[1] // n_head
    piece = half // 4

    def share(first, size):
        columns = lax.dynamic_slice_in_dim(whole, first, size, 1)
        return jnp.dot(attended, columns, preferred_element_type=jnp.float32)

    theirs = (1 - head_group) * half
    received = [
        lax.ppermute(share(theirs + part * piece, piece).astype(jnp.bfloat16), "head", [(0, 1), (1, 0)])
        for part in range(4)
    ]
    received = jnp.concatenate(received, axis=1).astype(jnp.float32)
    return (share(head_group * half, half) + received).astype(jnp.bfloat16)


def solution(mesh):
    in_specs = (
        P(("seq", "head"), None),
        P(("seq", "head"), None),
        P(("seq", "head"), None),
        P(None, "seq", None),
        P("head", "seq"),
    )
    out_specs = P("seq", "head")
    body = head_body if mesh.size == HEADS and mesh.shape["seq"] == 16 else generic_body
    return jax.shard_map(body, mesh=mesh, in_specs=in_specs, out_specs=out_specs, check_vma=False)
```

```python
import functools

import jax
import jax.numpy as jnp
from jax import lax
from jax.experimental import pallas as pl
from jax.experimental.pallas import tpu as pltpu
from jax.sharding import PartitionSpec as P

HEADS = 32
HD = 128
CLUSTERS = 128


def slot_table(block_ids, slot_depth):
    sub_rows = block_ids.shape[-1]
    onehot = (block_ids[..., None] == jnp.arange(CLUSTERS, dtype=jnp.int32)).astype(jnp.float32)
    lower = (jnp.arange(sub_rows)[:, None] >= jnp.arange(sub_rows)[None, :]).astype(jnp.float32)
    running = jnp.einsum("ts,abse->abte", lower, onehot)
    ranking = (jnp.sum(running * onehot, axis=-1) - 1.0).astype(jnp.int32)
    depth_hit = (ranking[..., None] == jnp.arange(slot_depth, dtype=jnp.int32)).astype(jnp.bfloat16)
    return onehot.astype(jnp.bfloat16)[..., :, None] * depth_hit[..., None, :]


def attend_blocks(packed, validity):
    scores = jnp.einsum(
        "cqd,ckd->cqk", packed[0], packed[1], preferred_element_type=jnp.float32
    ) * HD ** (-0.5)
    scores = jnp.where(validity[:, None, :] > 0, scores, -1e30)
    row_max = jnp.max(scores, axis=-1, keepdims=True)
    raised = jnp.exp(scores - row_max)
    weights = (raised / jnp.sum(raised, axis=-1, keepdims=True)).astype(jnp.bfloat16)
    return jnp.einsum(
        "cqk,ckd->cqd", weights, packed[2], preferred_element_type=jnp.float32
    ).astype(jnp.bfloat16)


def attend_and_return(arrived):
    packed, markers = arrived
    item_count = packed.shape[1]
    n_seq = packed.shape[2]
    lane_count = packed.shape[3]
    result_block = attend_blocks(
        packed.reshape(3, item_count, n_seq * lane_count, HD),
        markers.reshape(item_count, n_seq * lane_count),
    )
    result_block = result_block.reshape(item_count, n_seq, lane_count, HD)
    return lax.all_to_all(result_block, "seq", split_axis=1, concat_axis=1, tiled=True)


def generic_body(queries, keys, values, cluster_ids, out_weight):
    n_seq = lax.axis_size("seq")
    n_head = lax.axis_size("head")
    head_group = lax.axis_index("head")
    tok_dev = cluster_ids.shape[1]
    sub_rows = tok_dev // n_head
    group_heads = HEADS // n_head
    slot_depth = max(2, 2 * tok_dev // (n_head * CLUSTERS))
    lane_count = n_head * slot_depth
    per_owner = group_heads * CLUSTERS // n_seq
    all_ids = cluster_ids[:, :, 0]
    group_ids = lax.dynamic_slice_in_dim(all_ids, head_group * group_heads, group_heads, 0)
    group_ids = group_ids.reshape(group_heads, n_head, sub_rows)
    home_table = slot_table(group_ids, slot_depth)
    relaid = (
        lax.all_to_all(queries, "head", split_axis=1, concat_axis=0, tiled=True),
        lax.all_to_all(keys, "head", split_axis=1, concat_axis=0, tiled=True),
        lax.all_to_all(values, "head", split_axis=1, concat_axis=0, tiled=True),
    )
    stacked = jnp.stack([tensor.reshape(n_head, sub_rows, group_heads, HD) for tensor in relaid])
    packed = jnp.einsum(
        "hltcr,xlthd->xhclrd", home_table, stacked, preferred_element_type=jnp.float32
    ).astype(jnp.bfloat16)
    packed = packed.reshape(3, per_owner, n_seq, lane_count, HD)
    markers = (
        jnp.sum(home_table.astype(jnp.float32), axis=2).transpose(0, 2, 1, 3).astype(jnp.bfloat16)
    )
    markers = markers.reshape(1, per_owner, n_seq, lane_count)
    returned = attend_and_return(
        (
            lax.all_to_all(packed, "seq", split_axis=2, concat_axis=2, tiled=True),
            lax.all_to_all(markers, "seq", split_axis=2, concat_axis=2, tiled=True),
        )
    )
    returned = returned.reshape(group_heads, CLUSTERS, n_head, slot_depth, HD)
    gathered = jnp.einsum(
        "hltcr,hclrd->lthd", home_table, returned, preferred_element_type=jnp.float32
    ).astype(jnp.bfloat16)
    gathered = gathered.reshape(tok_dev, group_heads * HD)
    partial_value = jnp.dot(
        gathered,
        lax.all_gather(out_weight, "seq", axis=1, tiled=True),
        preferred_element_type=jnp.float32,
    )
    return lax.psum_scatter(
        partial_value.astype(jnp.bfloat16), "head", scatter_dimension=1, tiled=True
    )


GROUP = 16
CHUNK = 16


def flipped(index, mask, count):
    total, bit = 0, 1
    while bit < count:
        total = total + (index // bit + mask // bit) % 2 * bit
        bit *= 2
    return total


def attend_kernel(
    n_seq, n_head, most,
    q_ref, k_ref, v_ref, w_ref, code_ref, att_ref, whole_ref,
    recv, rcode, packed, marks, result, back,
    out_sem, in_sem, code_out, code_in, back_out, back_in, weight_out, weight_in,
):
    n_dev = n_seq * n_head
    per_group = GROUP // most
    n_group = n_dev // per_group
    sub = q_ref.shape[0]
    tok = n_head * sub
    wide = per_group * sub
    me_s, me_x = lax.axis_index("seq"), lax.axis_index("head")
    me = me_x * n_seq + me_s
    block = me_s * n_head + me_x
    my_group = block // per_group
    slots = CLUSTERS * GROUP

    def place(index):
        return {"seq": index % n_seq, "head": index // n_seq}

    def group_mask(step):
        return step % 2 * (n_group // 2) + step // 2

    def landing(source, part):
        rows = pl.ds(pl.multiple_of(source % per_group * sub, sub), sub)
        return recv.at[source // per_group, rows, part * HD:(part + 1) * HD]

    def code_landing(source):
        lanes = pl.ds(pl.multiple_of(source % per_group * sub, sub), sub)
        return rcode.at[source // per_group, :, lanes]

    def columns(index):
        return pl.ds(pl.multiple_of(index * HD, HD), HD)

    parts = (q_ref, k_ref, v_ref)

    barrier = pltpu.get_barrier_semaphore()

    def greet(step, carry):
        pl.semaphore_signal(
            barrier, inc=1, device_id=place((me + step) % n_dev), device_id_type=pl.DeviceIdType.MESH
        )
        return carry

    for part, ref in enumerate(parts):
        pltpu.make_async_copy(ref.at[:, columns(me)], landing(block, part), in_sem.at[part, block]).start()
    pltpu.make_async_copy(code_ref.at[me], code_landing(block), code_in.at[block]).start()
    lax.fori_loop(1, n_dev, greet, 0)
    pl.semaphore_wait(barrier, n_dev - 1)

    def target(step):
        inner = step % 4
        mask = group_mask(step // 4) * 2 + inner % 2 + inner // 2 * n_seq
        return flipped(me, mask, n_dev)

    def code_copy(dst):
        return pltpu.make_async_remote_copy(
            src_ref=code_ref.at[dst], dst_ref=code_landing(block),
            send_sem=code_out.at[dst], recv_sem=code_in.at[block],
            device_id=place(dst), device_id_type=pl.DeviceIdType.MESH,
        )

    def row_copy(dst, part):
        return pltpu.make_async_remote_copy(
            src_ref=parts[part].at[:, columns(dst)], dst_ref=landing(block, part),
            send_sem=out_sem.at[part, dst], recv_sem=in_sem.at[part, block],
            device_id=place(dst), device_id_type=pl.DeviceIdType.MESH,
        )

    def send(step, carry):
        dst = target(step)
        code_copy(dst).start()
        for part in range(3):
            row_copy(dst, part).start()
        return carry

    width = w_ref.shape[1]

    def weight_block(index):
        return whole_ref.at[:, pl.ds(pl.multiple_of(index * width, width), width)]

    def weight_copy(stage, item):
        mask = n_seq >> (stage + 1)
        held = flipped(me_s, item * (2 * mask), n_seq)
        return pltpu.make_async_remote_copy(
            src_ref=w_ref if stage == 0 else weight_block(held), dst_ref=weight_block(held),
            send_sem=weight_out.at[2 ** stage - 1 + item], recv_sem=weight_in.at[held],
            device_id={"seq": flipped(me_s, mask, n_seq), "head": me_x},
            device_id_type=pl.DeviceIdType.MESH,
        )

    stages = n_seq.bit_length() - 1

    def spread(stage):
        if stage > 0:
            weights_arrive(stage - 1)
        for item in range(2 ** stage):
            weight_copy(stage, item).start()

    def weights_arrive(stage):
        mask = n_seq >> (stage + 1)
        for item in range(2 ** stage):
            new = flipped(me_s, item * (2 * mask) + mask, n_seq)
            pltpu.make_async_copy(weight_block(new), weight_block(new), weight_in.at[new]).wait()

    own_weight = pltpu.make_async_copy(w_ref, weight_block(me_s), weight_in.at[me_s])
    own_weight.start()
    spread(0)
    lax.fori_loop(1, n_dev, send, 0)
    own_weight.wait()

    ones = jnp.ones((wide, HD), jnp.bfloat16)

    def pack_group(step, carry):
        group = flipped(my_group, group_mask(step), n_group)

        def arrive(inner, carry):
            source = group * per_group + inner
            pltpu.make_async_copy(code_landing(source), code_landing(source), code_in.at[source]).wait()
            for part in range(3):
                pltpu.make_async_copy(landing(source, part), landing(source, part), in_sem.at[part, source]).wait()
            return carry

        lax.fori_loop(0, per_group, arrive, 0)

        def pack_chunk(chunk, carry):
            rows = lax.broadcasted_iota(jnp.int32, (CHUNK * GROUP, wide), 0) + chunk * (CHUNK * GROUP)
            hit = jnp.where(rcode[group] == rows, 1.0, 0.0).astype(jnp.bfloat16)
            at = (
                pl.ds(chunk * CHUNK, CHUNK),
                pl.ds(pl.multiple_of(group * GROUP, GROUP), GROUP),
            )
            data = jnp.dot(hit, recv[group], preferred_element_type=jnp.float32).astype(jnp.bfloat16)
            packed[at[0], at[1], :] = data.reshape(CHUNK, GROUP, 3 * HD)
            mark = jnp.dot(hit, ones, preferred_element_type=jnp.float32).astype(jnp.bfloat16)
            marks[at[0], at[1], :] = mark.reshape(CHUNK, GROUP, HD)
            return carry

        return lax.fori_loop(0, CLUSTERS // CHUNK, pack_chunk, carry)

    lax.fori_loop(0, 2, pack_group, 0)
    spread(1)
    lax.fori_loop(2, 4, pack_group, 0)
    spread(2)
    lax.fori_loop(4, n_group, pack_group, 0)

    def attend(step, carry):
        for inner in range(4):
            cluster = step * 4 + inner
            scores = lax.dot_general(
                packed[cluster, :, HD:2 * HD], packed[cluster, :, 0:HD],
                (((1,), (1,)), ((), ())), preferred_element_type=jnp.float32,
            ) * HD ** (-0.5)
            scores = jnp.where(marks[cluster].astype(jnp.float32) > 0, scores, -1e30)
            raised = jnp.exp(scores - jnp.max(scores, axis=0, keepdims=True))
            weights = (raised / jnp.sum(raised, axis=0, keepdims=True)).astype(jnp.bfloat16)
            result[cluster] = lax.dot_general(
                weights, packed[cluster, :, 2 * HD:3 * HD],
                (((0,), (0,)), ((), ())), preferred_element_type=jnp.float32,
            ).astype(jnp.bfloat16)
        return carry

    lax.fori_loop(0, CLUSTERS // 4, attend, 0)
    spread(3)

    seqs = per_group // n_head

    def back_copy(group, part):
        dst = group * seqs + part
        return pltpu.make_async_remote_copy(
            src_ref=back.at[group, part * tok:(part + 1) * tok, :], dst_ref=att_ref.at[:, columns(me_s)],
            send_sem=back_out.at[dst], recv_sem=back_in.at[me_s],
            device_id={"seq": dst, "head": me_x}, device_id_type=pl.DeviceIdType.MESH,
        )

    def unpack(group):
        rows = result[:, pl.ds(pl.multiple_of(group * GROUP, GROUP), GROUP), :].reshape(slots, HD)
        for part in range(seqs):
            lanes = slice(part * tok, (part + 1) * tok)
            hit = rcode[group, :, lanes] == lax.broadcasted_iota(jnp.int32, (slots, tok), 0)
            hit = jnp.where(hit, 1.0, 0.0).astype(jnp.bfloat16)
            turned = lax.dot_general(
                rows, hit, (((0,), (0,)), ((), ())), preferred_element_type=jnp.float32
            )
            back[group, lanes, :] = turned.T.astype(jnp.bfloat16)

    def send_back(step, carry):
        group = flipped(my_group, group_mask(n_group - step), n_group)
        unpack(group)
        for part in range(seqs):
            back_copy(group, part).start()
        return carry

    lax.fori_loop(1, n_group, send_back, 0)
    unpack(my_group)
    own = me_s % seqs
    own_rows = pl.ds(pl.multiple_of(own * tok, tok), tok)
    local = pltpu.make_async_copy(back.at[my_group, own_rows, :], att_ref.at[:, columns(me_s)], back_in.at[me_s])
    local.start()

    def send_near(step, carry):
        part = (own + step) % seqs
        dst = my_group * seqs + part
        pltpu.make_async_remote_copy(
            src_ref=back.at[my_group, pl.ds(pl.multiple_of(part * tok, tok), tok), :],
            dst_ref=att_ref.at[:, columns(me_s)],
            send_sem=back_out.at[dst], recv_sem=back_in.at[me_s],
            device_id={"seq": dst, "head": me_x}, device_id_type=pl.DeviceIdType.MESH,
        ).start()
        return carry

    lax.fori_loop(1, seqs, send_near, 0)

    def finish_sends(step, carry):
        dst = target(step)
        code_copy(dst).wait_send()
        for part in range(3):
            row_copy(dst, part).wait_send()
        return carry

    lax.fori_loop(1, n_dev, finish_sends, 0)
    local.wait()

    def finish_back(step, carry):
        other = (me_s + step) % n_seq
        landed = att_ref.at[:, columns(other)]
        pltpu.make_async_copy(landed, landed, back_in.at[other]).wait()
        left = back.at[other // seqs, pl.ds(pl.multiple_of(other % seqs * tok, tok), tok), :]
        pltpu.make_async_copy(left, left, back_out.at[other]).wait()
        return carry

    lax.fori_loop(1, n_seq, finish_back, 0)
    weights_arrive(stages - 1)
    for stage in range(stages):
        for item in range(2 ** stage):
            weight_copy(stage, item).wait_send()


def head_body(queries, keys, values, cluster_ids, out_weight):
    n_seq = lax.axis_size("seq")
    n_head = lax.axis_size("head")
    n_dev = n_seq * n_head
    tok_dev = cluster_ids.shape[1]
    sub_rows = tok_dev // n_head
    group_heads = HEADS // n_head
    most = max(2, 2 * tok_dev // (n_head * CLUSTERS))
    per_group = GROUP // most
    n_group = n_dev // per_group
    wide = per_group * sub_rows
    head_group = lax.axis_index("head")
    block = lax.axis_index("seq") * n_head + head_group
    ids = lax.dynamic_slice_in_dim(cluster_ids[:, :, 0], head_group * sub_rows, sub_rows, 1)
    earlier = jnp.arange(sub_rows)[:, None] < jnp.arange(sub_rows)[None, :]
    same = (ids[:, :, None] == ids[:, None, :]) & earlier[None]
    ranking = jnp.sum(same.astype(jnp.int32), axis=1)
    codes = ids * GROUP + (block % per_group) * most + ranking
    codes = codes.reshape(HEADS, 1, sub_rows)
    anywhere = pl.BlockSpec(memory_space=pl.ANY)
    attended, whole = pl.pallas_call(
        functools.partial(attend_kernel, n_seq, n_head, most),
        out_shape=(
            jax.ShapeDtypeStruct((tok_dev, group_heads * HD), jnp.bfloat16),
            jax.ShapeDtypeStruct((out_weight.shape[0], n_seq * out_weight.shape[1]), jnp.bfloat16),
        ),
        in_specs=[anywhere, anywhere, anywhere, anywhere, pl.BlockSpec(memory_space=pltpu.VMEM)],
        out_specs=(anywhere, anywhere),
        scratch_shapes=[
            pltpu.VMEM((n_group, wide, 3 * HD), jnp.bfloat16),
            pltpu.VMEM((n_group, 1, wide), jnp.int32),
            pltpu.VMEM((CLUSTERS, n_group * GROUP, 3 * HD), jnp.bfloat16),
            pltpu.VMEM((CLUSTERS, n_group * GROUP, HD), jnp.bfloat16),
            pltpu.VMEM((CLUSTERS, n_group * GROUP, HD), jnp.bfloat16),
            pltpu.VMEM((n_group, wide, HD), jnp.bfloat16),
            pltpu.SemaphoreType.DMA((3, n_dev)),
            pltpu.SemaphoreType.DMA((3, n_dev)),
            pltpu.SemaphoreType.DMA((n_dev,)),
            pltpu.SemaphoreType.DMA((n_dev,)),
            pltpu.SemaphoreType.DMA((n_seq,)),
            pltpu.SemaphoreType.DMA((n_seq,)),
            pltpu.SemaphoreType.DMA((n_seq,)),
            pltpu.SemaphoreType.DMA((n_seq,)),
        ],
        compiler_params=pltpu.CompilerParams(
            collective_id=0, has_side_effects=True, vmem_limit_bytes=56 * 2 ** 20
        ),
        cost_estimate=pl.CostEstimate(flops=2 * 10 ** 10, bytes_accessed=2 * 10 ** 7, transcendentals=2 ** 21),
    )(queries, keys, values, out_weight, codes)
    half = whole.shape[1] // n_head
    piece = half // 4

    def share(first, size):
        columns = lax.dynamic_slice_in_dim(whole, first, size, 1)
        return jnp.dot(attended, columns, preferred_element_type=jnp.float32)

    theirs = (1 - head_group) * half
    received = [
        lax.ppermute(share(theirs + part * piece, piece).astype(jnp.bfloat16), "head", [(0, 1), (1, 0)])
        for part in range(4)
    ]
    own = lax.optimization_barrier(share(head_group * half, half))
    received = jnp.concatenate(received, axis=1).astype(jnp.float32)
    return (own + received).astype(jnp.bfloat16)


def solution(mesh):
    in_specs = (
        P(("seq", "head"), None),
        P(("seq", "head"), None),
        P(("seq", "head"), None),
        P(None, "seq", None),
        P("head", "seq"),
    )
    out_specs = P("seq", "head")
    body = head_body if mesh.size == HEADS and mesh.shape["seq"] == 16 else generic_body
    return jax.shard_map(body, mesh=mesh, in_specs=in_specs, out_specs=out_specs, check_vma=False)
```
